768 devices in a mesh: node: 32 (over x_lo, y, core), feat: 24 (over x_hi, z).
Axes of the slice: x: 4 (x_hi: 2, x_lo: 2; x = x_hi * 2 + x_lo), y: 8, z: 12, core: 2. Of those that a mesh axis runs over, the one named last changes fastest.
Arguments:
- features: bfloat16 [196608, 192], P(('node', 'feat')), may hold values from -6 to 6
- cotangent: bfloat16 [196608, 192], P(('node', 'feat')), may hold values from -6 to 6
- w_self: bfloat16 [192, 192], replicated, may hold values from -0.4375 to 0.4375
- w_neigh: bfloat16 [192, 192], replicated, may hold values from -0.4375 to 0.4375
- degree: int32 [196608], P(('node', 'feat')), may hold values from 4 to 63
- tile_row: int32 [8192], P('node'), may hold values from 0 to 23
- tile_col: int32 [8192], P('node'), may hold values from 0 to 767
- tile_fill: int32 [8192], P('node'), may hold values from 0 to 64, as said below
Outputs:
- input_grad: bfloat16 [196608, 192], P(('node', 'feat'))
- self_grad: float32 [192, 192], replicated
- neigh_grad: float32 [192, 192], replicated
The draws below stay inside these ranges and needn't reach their ends.
Inputs may be any that keep to these rules, and one draw needn't show every extreme that they name: `tile_fill`: in each node group's 256 slots the nonzero values come first; a zero slot holds no edge; every group has at least 64 nonzero slots, and some group has all 256.
All inputs are finite; a program needn't handle non-finite values.
Results may differ from the reference program's by a relative error of at most 0.0047.
Values may be sent and summed in bfloat16 or wider, within the bound.
A program may use at most 32 MiB of HBM per device.

```python
import math
import jax
import jax.numpy as jnp
from jax import lax

F = 192
TILE = 256
TCAP = 256
NODES = 196608
BT = 24
NT = 768
N_NODE = 32


def draw_tile_fill(key, part):
    key = jax.random.fold_in(key, 5)
    key_live, key_full, key_vals = jax.random.split(key, 3)
    group_count = N_NODE
    live_count = jax.random.randint(key_live, (group_count,), TCAP // 4, TCAP + 1)
    full_group = jax.random.randint(key_full, (), 0, group_count)
    group_ids = jnp.arange(group_count)
    live_count = jnp.where(group_ids == (full_group + 1) % group_count, TCAP // 4, live_count)
    live_count = jnp.where(group_ids == full_group, TCAP, live_count)
    values = jax.random.randint(key_vals, (group_count, TCAP), 1, 65)
    values = values.at[full_group, 0].set(64)
    slot_ids = jnp.arange(TCAP)[None, :]
    return jnp.where(slot_ids < live_count[:, None], values, 0).reshape(-1).astype(jnp.int32)


def place_ends(entries, stream_key, least, top_value):
    extent = entries.shape
    index_at = [jax.random.randint(jax.random.fold_in(stream_key, axis), (), 0, extent[axis]) for axis in range(len(extent))]
    entries = entries.at[tuple(index_at)].set(least)
    longest = extent.index(max(extent))
    index_at[longest] = (index_at[longest] + 1) % extent[longest]
    return entries.at[tuple(index_at)].set(top_value)


def steps_of(stream_key, shape, shards, least, top_value):
    def one(dim, parts):
        heights = jax.random.uniform(jax.random.fold_in(jax.random.fold_in(stream_key, 6), dim), (parts,), jnp.float32, least / len(shards), top_value / len(shards))
        return jnp.repeat(jnp.exp(heights), shape[dim] // parts).reshape((-1,) + (1,) * (len(shape) - dim - 1))

    level = one(*shards[0])
    for cut in shards[1:]:
        level = level * one(*cut)
    return level


def centred(stream_key, dims, spread, limit, shards=(), kind=jnp.bfloat16):
    drawn = spread * jax.random.normal(stream_key, dims, jnp.float32)
    if shards:
        drawn = drawn * steps_of(stream_key, dims, shards, -0.22, 0.18)
    return jnp.clip(drawn, -limit, limit).astype(kind)


def setup_inputs(seed: int = 0) -> dict:
    keys = jax.random.split(jax.random.key(seed), 9)
    return {
        "features": centred(keys[0], (NODES, F), 1.0, 6.0, ((0, 768),)),
        "cotangent": centred(keys[1], (NODES, F), 1.0, 6.0, ((0, 768),)),
        "w_self": centred(keys[2], (F, F), F ** -0.5, 0.4375),
        "w_neigh": centred(keys[3], (F, F), F ** -0.5, 0.4375),
        "degree": place_ends(jax.random.randint(keys[4], (NODES,), 4, 64), jax.random.fold_in(keys[4], 1), 4, 63).astype(jnp.int32),
        "tile_row": place_ends(jax.random.randint(keys[5], (N_NODE * TCAP,), 0, BT), jax.random.fold_in(keys[5], 1), 0, BT - 1).astype(jnp.int32),
        "tile_col": place_ends(jax.random.randint(keys[6], (N_NODE * TCAP,), 0, NT), jax.random.fold_in(keys[6], 1), 0, NT - 1).astype(jnp.int32),
        "tile_fill": draw_tile_fill(jax.random.fold_in(keys[8], 71), 0),
    }


def tile_pattern(fill_values, seed_values, tile_size):
    rows_idx = lax.broadcasted_iota(jnp.int32, (1, tile_size, tile_size), 1)
    cols_idx = lax.broadcasted_iota(jnp.int32, (1, tile_size, tile_size), 2)
    residue = (13 * rows_idx * rows_idx + 7 * rows_idx * cols_idx + 197 * cols_idx + 31 * seed_values[:, None, None]) % 251
    return (residue < fill_values[:, None, None]).astype(jnp.float32)

def reference(features, cotangent, w_self, w_neigh, degree, tile_row, tile_col, tile_fill):
    node_total = features.shape[0]
    scaled = (cotangent.astype(jnp.float32) / degree[:, None].astype(jnp.float32)).astype(jnp.bfloat16)
    slot_count = tile_fill.shape[0]
    slot_ids = jnp.arange(slot_count, dtype=jnp.int32)
    global_row = slot_ids // TCAP * BT + tile_row
    offsets = jnp.arange(TILE, dtype=jnp.int32)

    def panel_step(running, chosen):
        pattern = tile_pattern(tile_fill[chosen], chosen, TILE)
        source_rows = (global_row[chosen][:, None] * TILE + offsets[None, :]).reshape(-1)
        sources = scaled[source_rows].astype(jnp.float32).reshape(chosen.shape[0], TILE, F)
        products = jnp.einsum('prs,prf->psf', pattern, sources)
        target_rows = (tile_col[chosen][:, None] * TILE + offsets[None, :]).reshape(-1)
        return (running.at[target_rows].add(products.reshape(-1, F)), None)
    summed, _ = lax.scan(panel_step, jnp.zeros((node_total, F), jnp.float32), slot_ids.reshape(-1, 32))
    gathered = summed.astype(jnp.bfloat16)
    input_grad = (jnp.dot(cotangent, w_self.T, preferred_element_type=jnp.float32) + jnp.dot(gathered, w_neigh.T, preferred_element_type=jnp.float32)).astype(jnp.bfloat16)
    factor_norm = 1.0 / math.sqrt(NODES)
    self_grad = jnp.dot(features.T, cotangent, preferred_element_type=jnp.float32) * factor_norm
    neigh_grad = jnp.dot(features.T, gathered, preferred_element_type=jnp.float32) * factor_norm
    return (input_grad, self_grad, neigh_grad)
```

```python
import functools
import math

import jax
import jax.numpy as jnp
from jax import lax
from jax.experimental import pallas as pl
from jax.experimental.pallas import tpu as pltpu
from jax.sharding import PartitionSpec as P

TILE = 256
HALF = TILE // 2
WIDTH = 8
MOD = 251
UNROLL = 4
MESH = pl.DeviceIdType.MESH
F32 = jnp.float32
BF16 = jnp.bfloat16


def node_coords(node_y):
    me = lax.axis_index("node")
    core = lax.rem(me, 2)
    y = lax.rem(lax.div(me, 2), node_y)
    x = lax.div(me, 2 * node_y)
    return x, y, core


def greet(n_node, n_feat):
    me_n, me_f = lax.axis_index("node"), lax.axis_index("feat")
    barrier = pltpu.get_barrier_semaphore()

    def feat_peer(k, _):
        pl.semaphore_signal(
            barrier, inc=1, device_id={"feat": lax.rem(me_f + k, n_feat)}, device_id_type=MESH
        )
        return 0

    def node_peer(k, _):
        pl.semaphore_signal(
            barrier, inc=1, device_id={"node": lax.rem(me_n + k, n_node)}, device_id_type=MESH
        )
        return 0

    lax.fori_loop(1, n_feat, feat_peer, 0)
    lax.fori_loop(1, n_node, node_peer, 0)
    return barrier, n_feat + n_node - 2


def spread(axis, count, src_of, dst, send_sem, recv_sem):
    me = lax.axis_index(axis)

    def one(k, _):
        peer = lax.rem(me + k, count)
        pltpu.make_async_remote_copy(
            src_ref=src_of(peer),
            dst_ref=dst,
            send_sem=send_sem,
            recv_sem=recv_sem,
            device_id={axis: peer},
            device_id_type=MESH,
        ).start()
        return 0

    lax.fori_loop(1, count, one, 0)


def wait_bytes(view, sem):
    pltpu.make_async_copy(view, view, sem).wait()


class GradSum:
    def __init__(self, n_node, n_feat, local, by_feat, chunk, by_node, out, sems):
        self.n_node, self.n_feat = n_node, n_feat
        self.local, self.by_feat, self.chunk, self.by_node, self.out = (
            local, by_feat, chunk, by_node, out,
        )
        self.sems = sems

    def feat_start(self):
        me = lax.axis_index("feat")
        spread("feat", self.n_feat, lambda p: self.local.at[p], self.by_feat.at[me],
               self.sems.at[0], self.sems.at[1])
        self.by_feat[me] = self.local[me]

    def node_start(self):
        wait_bytes(self.by_feat.at[pl.ds(0, self.n_feat - 1)], self.sems.at[1])
        me = lax.axis_index("node")
        total = jnp.sum(self.by_feat[...], axis=0)
        self.chunk[...] = total
        spread("node", self.n_node, lambda p: self.chunk, self.by_node.at[me],
               self.sems.at[2], self.sems.at[3])
        self.by_node[me] = total

    def back_start(self, factor):
        wait_bytes(self.by_node.at[pl.ds(0, self.n_node - 1)], self.sems.at[3])
        me = lax.axis_index("feat")
        self.out[me] = jnp.sum(self.by_node[...], axis=0) * factor
        spread("feat", self.n_feat, lambda p: self.out.at[me], self.out.at[me],
               self.sems.at[4], self.sems.at[5])

    def finish(self):
        wait_bytes(self.out.at[pl.ds(0, self.n_feat - 1)], self.sems.at[5])
        wait_bytes(self.local.at[pl.ds(0, self.n_feat - 1)], self.sems.at[0])
        wait_bytes(self.by_node.at[pl.ds(0, self.n_node - 1)], self.sems.at[2])
        wait_bytes(self.out.at[pl.ds(0, self.n_feat - 1)], self.sems.at[4])


def grad_scratch(n_node, n_feat, width):
    return [
        pltpu.VMEM((n_feat, WIDTH, width), F32),
        pltpu.VMEM((n_feat, WIDTH, width), F32),
        pltpu.VMEM((WIDTH, width), F32),
        pltpu.VMEM((n_node, WIDTH, width), F32),
        pltpu.SemaphoreType.DMA((6,)),
    ]


def slot_table(n_node, n_feat, row, col, fill):
    me = lax.axis_index("node")
    slot = lax.broadcasted_iota(jnp.int32, (1, TILE), 1)
    shift = lax.rem(31 * (me * TILE + slot), MOD)
    low = jnp.where(shift == 0, 0, MOD - shift)
    bound = jnp.where(fill > 0, fill + jnp.where(low + fill > MOD, 256 - MOD, 0), 0)
    group = lax.div(col, n_feat)
    member = col - group * n_feat
    key = (jnp.where(fill > 0, group, n_node) * TILE + slot).astype(F32)
    keys = jnp.broadcast_to(key, (TILE, TILE))
    keys_t = keys.T
    rank = jnp.sum((keys_t < keys).astype(F32), axis=0, keepdims=True)
    place = lax.broadcasted_iota(jnp.int32, (TILE, TILE), 0).astype(F32)
    chosen = (place == rank).astype(F32).astype(BF16)
    line = lax.broadcasted_iota(jnp.int32, (8, TILE), 0)
    which = lax.rem(line, 4)
    payload = jnp.where(
        which == 0, low, jnp.where(which == 1, bound, jnp.where(which == 2, row, member))
    ).astype(F32).astype(BF16)
    ordered = lax.dot_general(
        payload, chosen, (((1,), (1,)), ((), ())), preferred_element_type=F32
    )
    head = jnp.where(line[:, :HALF] < 4, ordered[:, :HALF], ordered[:, HALF:])
    edge = (lax.broadcasted_iota(jnp.int32, (1, HALF), 1) * TILE).astype(F32)
    before = jnp.sum((keys_t[:, :HALF] < edge).astype(F32), axis=0, keepdims=True)
    return jnp.concatenate([head, jnp.broadcast_to(before, (8, HALF))], axis=0).astype(BF16)


def exchange_kernel(
    n_node, n_feat, factor,
    feat_ref, cot_ref, deg_ref, row_ref, col_ref, fill_ref,
    blocks, self_out,
    send, g_local, g_feat, g_chunk, g_node, g_sems, a_sems, ring_sems, end_sems,
):
    node_y = n_node // 4
    span = n_feat + 1
    cut = (span * 11) // 25
    x, y, core = node_coords(node_y)
    me_n, me_f = lax.axis_index("node"), lax.axis_index("feat")
    barrier, expected = greet(n_node, n_feat)

    scaled = cot_ref[...].astype(F32).T / deg_ref[...].astype(F32)
    for j in range(n_feat):
        part = scaled[j * WIDTH:(j + 1) * WIDTH]
        send[j] = jnp.concatenate([part[:, :HALF], part[:, HALF:]], axis=0).astype(BF16)
    home = me_n * span
    blocks[home + me_f] = send[me_f]
    pl.semaphore_wait(barrier, expected)
    spread("feat", n_feat, lambda p: send.at[p], blocks.at[home + me_f], a_sems.at[0], a_sems.at[1])

    blocks[home + n_feat] = slot_table(n_node, n_feat, row_ref[...], col_ref[...], fill_ref[...])
    grads = GradSum(n_node, n_feat, g_local, g_feat, g_chunk, g_node, self_out, g_sems)
    g_local[...] = lax.dot_general(
        feat_ref[...], cot_ref[...], (((0,), (0,)), ((), ())), preferred_element_type=F32
    ).reshape(g_local.shape)
    wait_bytes(send.at[pl.ds(0, n_feat - 1)], a_sems.at[1])

    def node_at(xx, yy, cc):
        return (xx * node_y + yy) * 2 + cc

    def view(side, offset, lo, hi):
        xx = x if side == 0 else 1 - x
        yy = lax.rem(y + offset + node_y, node_y)
        return blocks.at[pl.ds(node_at(xx, yy, core) * span + lo, hi - lo)]

    ids = {}

    def move(name, ref, target):
        number = ids.setdefault(name, len(ids))
        pltpu.make_async_remote_copy(
            src_ref=ref, dst_ref=ref, send_sem=end_sems.at[0], recv_sem=ring_sems.at[number],
            device_id={"node": target}, device_id_type=MESH,
        ).start()
        return number

    sent = [0]

    def to_sibling(ref):
        pltpu.make_async_remote_copy(
            src_ref=ref, dst_ref=ref, send_sem=end_sems.at[1], recv_sem=end_sems.at[2],
            device_id={"node": node_at(x, y, 1 - core)}, device_id_type=MESH,
        ).start()

    half = node_y // 2
    near = [(0, cut, span), (0, 0, cut), (1, 0, cut)]
    room = (span + cut) // 2
    far = {1: [(0, cut, room), (0, 0, cut)], -1: [(0, room, span), (1, 0, cut)]}

    def pieces(step, way):
        return near if step < half else far[way]

    def pass_on(step, way, side, lo, hi):
        if step >= half:
            return
        for s2, lo2, hi2 in pieces(step + 1, way):
            if s2 == side and lo2 >= lo and hi2 <= hi:
                target = node_at(x, lax.rem(y + way + node_y, node_y), core)
                move(("y", way, step + 1, s2, lo2), view(side, -way * step, lo2, hi2), target)
                sent[0] += hi2 - lo2

    partner = node_at(1 - x, y, core)

    def to_partner(name, ref, count):
        move(name, ref, partner)
        sent[0] += count

    pending = []
    for side, lo, hi in near[:2]:
        for way in (1, -1):
            pass_on(0, way, side, lo, hi)
        to_partner(("x", 0, 0, lo), view(0, 0, lo, hi), hi - lo)
    to_sibling(view(0, 0, 0, span))
    grads.feat_start()
    wait_bytes(view(1, 0, 0, cut), ring_sems.at[ids[("x", 0, 0, 0)]])
    for way in (1, -1):
        pass_on(0, way, 1, 0, cut)
    to_sibling(view(1, 0, 0, cut))
    pending.append((("x", 0, 0, cut), 0, cut, span))

    for step in range(1, half + 1):
        fresh = []
        for (right, left) in zip(pieces(step, 1), pieces(step, -1)):
            for way, (side, lo, hi) in ((1, right), (-1, left)):
                ref = view(side, -way * step, lo, hi)
                wait_bytes(ref, ring_sems.at[ids[("y", way, step, side, lo)]])
                pass_on(step, way, side, lo, hi)
                if side == 0 and lo >= cut:
                    name = ("x", way, step, lo)
                    to_partner(name, ref, hi - lo)
                    fresh.append((name, -way * step, lo, hi))
                to_sibling(ref)
        for name, offset, lo, hi in pending:
            ref = view(1, offset, lo, hi)
            wait_bytes(ref, ring_sems.at[ids[name]])
            to_sibling(ref)
        pending = fresh
        if step == 1:
            grads.node_start()
        if step == half - 1:
            grads.back_start(factor)
    for name, offset, lo, hi in pending:
        ref = view(1, offset, lo, hi)
        wait_bytes(ref, ring_sems.at[ids[name]])
        to_sibling(ref)
    grads.finish()
    wait_bytes(send.at[pl.ds(0, n_feat - 1)], a_sems.at[0])
    wait_bytes(blocks.at[pl.ds(0, n_node // 2 * span)], end_sems.at[2])
    wait_bytes(blocks.at[pl.ds(0, n_node // 2 * span)], end_sems.at[1])
    wait_bytes(blocks.at[pl.ds(0, sent[0])], end_sems.at[0])


def slots_kernel(n_node, n_feat, blocks, out, acc, base, packed, before, packed_s, before_s, todo, sems):
    span = n_feat + 1
    me = lax.axis_index("node")

    table = blocks[...].reshape(n_node, span, 16, HALF)[:, n_feat].astype(F32).astype(jnp.int32)
    for k in range(2):
        low = table[:, 4 * k, :]
        bound = table[:, 4 * k + 1, :]
        row = table[:, 4 * k + 2, :]
        member = table[:, 4 * k + 3, :]
        first = lax.broadcasted_iota(jnp.int32, (n_node, HALF), 0) * span
        packed[k] = (first + row) + low * 1024 + bound * (1 << 18) + member * (1 << 25)
    before[...] = table[:, 8, :]
    moves = [
        pltpu.make_async_copy(packed, packed_s, sems.at[0]),
        pltpu.make_async_copy(before, before_s, sems.at[1]),
    ]
    for one in moves:
        one.start()

    r = lax.broadcasted_iota(jnp.int32, (TILE, TILE), 0)
    c = lax.broadcasted_iota(jnp.int32, (TILE, TILE), 1)
    residue = lax.rem(13 * r * r + 7 * r * c + 197 * c, MOD)
    base[...] = (residue * 256 - 32768).astype(jnp.int16)
    acc[...] = jnp.zeros_like(acc)
    for one in moves:
        one.wait()

    def collect_group(g, count):
        start, stop = before_s[g, me], before_s[g, me + 1]

        def put(i, at):
            todo[at] = packed_s[lax.div(i, HALF), g, lax.rem(i, HALF)]
            return at + 1

        return lax.fori_loop(start, stop, put, count)

    count = lax.fori_loop(0, n_node, collect_group, 0)
    for k in range(UNROLL - 1):
        todo[count + k] = 0

    def turn(i, _):
        for k in range(UNROLL):
            entry = todo[i * UNROLL + k]
            place = jnp.bitwise_and(entry, 1023)
            low = jnp.bitwise_and(lax.shift_right_logical(entry, 10), 255)
            bound = jnp.bitwise_and(lax.shift_right_logical(entry, 18), 127)
            member = lax.shift_right_logical(entry, 25)
            pair = blocks[place].astype(F32)
            source = jnp.concatenate([pair[:8], pair[8:]], axis=1).astype(BF16)
            moved = base[...] - jnp.full((TILE, TILE), low * 256, jnp.int32).astype(jnp.int16)
            limit = jnp.full((TILE, TILE), bound * 256 - 32768, jnp.int32).astype(jnp.int16)
            pattern = jnp.where(moved < limit, jnp.ones((), BF16), jnp.zeros((), BF16))
            acc[member] += jnp.dot(source, pattern, preferred_element_type=F32)
        return 0

    lax.fori_loop(0, lax.div(count + UNROLL - 1, UNROLL), turn, 0)
    for m in range(n_feat):
        part = acc[m]
        out[m] = jnp.concatenate([part[:, :HALF], part[:, HALF:]], axis=0).astype(BF16)


def finish_kernel(
    n_node, n_feat, factor,
    slices, feat_ref, cot_ref, w_self, w_neigh,
    grad_out, neigh_out,
    own, landed, g_local, g_feat, g_chunk, g_node, g_sems, a_sems,
):
    me_f = lax.axis_index("feat")
    barrier, expected = greet(n_node, n_feat)
    own[...] = lax.dot_general(
        cot_ref[...], w_self[...], (((1,), (1,)), ((), ())), preferred_element_type=F32
    )
    landed[me_f] = slices[me_f]
    pl.semaphore_wait(barrier, expected)
    spread("feat", n_feat, lambda p: slices.at[p], landed.at[me_f], a_sems.at[0], a_sems.at[1])
    wait_bytes(landed.at[pl.ds(0, n_feat - 1)], a_sems.at[1])
    parts = landed[...].astype(F32)
    gathered_t = jnp.concatenate([parts[:, :8], parts[:, 8:]], axis=2).reshape(n_feat * WIDTH, TILE)
    gathered = gathered_t.T.astype(BF16)
    grads = GradSum(n_node, n_feat, g_local, g_feat, g_chunk, g_node, neigh_out, g_sems)
    g_local[...] = lax.dot_general(
        feat_ref[...], gathered, (((0,), (0,)), ((), ())), preferred_element_type=F32
    ).reshape(g_local.shape)
    grads.feat_start()
    grad_out[...] = (
        own[...]
        + lax.dot_general(
            gathered, w_neigh[...], (((1,), (1,)), ((), ())), preferred_element_type=F32
        )
    ).astype(BF16)
    grads.node_start()
    grads.back_start(factor)
    grads.finish()
    wait_bytes(slices.at[pl.ds(0, n_feat - 1)], a_sems.at[0])


def in_vmem(count):
    return [pl.BlockSpec(memory_space=pltpu.VMEM)] * count


def local(n_node, n_feat, features, cotangent, w_self, w_neigh, degree, tile_row, tile_col, tile_fill):
    width = n_feat * WIDTH
    span = n_feat + 1
    factor = 1.0 / math.sqrt(n_node * n_feat * TILE)
    line = (1, TILE)
    blocks, self_grad = pl.pallas_call(
        functools.partial(exchange_kernel, n_node, n_feat, factor),
        out_shape=(
            jax.ShapeDtypeStruct((n_node * span, 16, HALF), BF16),
            jax.ShapeDtypeStruct((n_feat, WIDTH, width), F32),
        ),
        in_specs=in_vmem(6),
        out_specs=tuple(in_vmem(2)),
        scratch_shapes=[
            pltpu.VMEM((n_feat, 16, HALF), BF16),
            *grad_scratch(n_node, n_feat, width),
            pltpu.SemaphoreType.DMA((2,)),
            pltpu.SemaphoreType.DMA((64,)),
            pltpu.SemaphoreType.DMA((3,)),
        ],
        compiler_params=pltpu.CompilerParams(
            collective_id=0, has_side_effects=True, vmem_limit_bytes=32 << 20
        ),
        name="exchange",
    )(
        features, cotangent, degree.reshape(line), tile_row.reshape(line),
        tile_col.reshape(line), tile_fill.reshape(line),
    )
    slices = pl.pallas_call(
        functools.partial(slots_kernel, n_node, n_feat),
        out_shape=jax.ShapeDtypeStruct((n_feat, 16, HALF), BF16),
        in_specs=in_vmem(1),
        out_specs=in_vmem(1)[0],
        scratch_shapes=[
            pltpu.VMEM((n_feat, WIDTH, TILE), F32),
            pltpu.VMEM((TILE, TILE), jnp.int16),
            pltpu.VMEM((2, n_node, HALF), jnp.int32),
            pltpu.VMEM((n_node, HALF), jnp.int32),
            pltpu.SMEM((2, n_node, HALF), jnp.int32),
            pltpu.SMEM((n_node, HALF), jnp.int32),
            pltpu.SMEM((n_node * TILE + UNROLL,), jnp.int32),
            pltpu.SemaphoreType.DMA((2,)),
        ],
        compiler_params=pltpu.CompilerParams(vmem_limit_bytes=32 << 20),
        name="slots",
    )(blocks)
    input_grad, neigh_grad = pl.pallas_call(
        functools.partial(finish_kernel, n_node, n_feat, factor),
        out_shape=(
            jax.ShapeDtypeStruct((TILE, width), BF16),
            jax.ShapeDtypeStruct((n_feat, WIDTH, width), F32),
        ),
        in_specs=in_vmem(5),
        out_specs=tuple(in_vmem(2)),
        scratch_shapes=[
            pltpu.VMEM((TILE, width), F32),
            pltpu.VMEM((n_feat, 16, HALF), BF16),
            *grad_scratch(n_node, n_feat, width),
            pltpu.SemaphoreType.DMA((2,)),
        ],
        compiler_params=pltpu.CompilerParams(
            collective_id=1, has_side_effects=True, vmem_limit_bytes=32 << 20
        ),
        name="finish",
    )(slices, features, cotangent, w_self, w_neigh)
    return input_grad, self_grad.reshape(width, width), neigh_grad.reshape(width, width)


def solution(mesh):
    n_node, n_feat = mesh.shape["node"], mesh.shape["feat"]
    return jax.shard_map(
        functools.partial(local, n_node, n_feat),
        mesh=mesh,
        in_specs=(
            P(("node", "feat"), None),
            P(("node", "feat"), None),
            P(),
            P(),
            P(("node", "feat")),
            P("node"),
            P("node"),
            P("node"),
        ),
        out_specs=(P(("node", "feat"), None), P(), P()),
        check_vma=False,
    )
```

```python
import functools
import math

import jax
import jax.numpy as jnp
from jax import lax
from jax.experimental import pallas as pl
from jax.experimental.pallas import tpu as pltpu
from jax.sharding import PartitionSpec as P

TILE = 256
HALF = TILE // 2
WIDTH = 8
MOD = 251
UNROLL = 16
MESH = pl.DeviceIdType.MESH
F32 = jnp.float32
BF16 = jnp.bfloat16


def node_coords(node_y):
    me = lax.axis_index("node")
    core = lax.rem(me, 2)
    y = lax.rem(lax.div(me, 2), node_y)
    x = lax.div(me, 2 * node_y)
    return x, y, core


def wrap(value, size):
    return lax.rem(value + size, size)


def far_step(t, size):
    back = lax.div(t + 1, 2)
    return lax.rem(size // 2 + jnp.where(lax.rem(t, 2) == 1, size - back, back), size)


def each_feat(n_feat, act):
    ring = n_feat // 2
    me = lax.axis_index("feat")
    hi, z = lax.div(me, ring), lax.rem(me, ring)

    def one(t, _):
        zz = lax.rem(z + far_step(t, ring), ring)
        act((1 - hi) * ring + zz)
        act(hi * ring + zz)
        return 0

    lax.fori_loop(0, ring - 1, one, 0)
    act((1 - hi) * ring + z)


def each_node(n_node, act):
    ring = n_node // 4
    x, y, core = node_coords(ring)

    def one(t, _):
        yy = lax.rem(y + far_step(t, ring), ring)
        act(((1 - x) * ring + yy) * 2 + 1 - core)
        act(((1 - x) * ring + yy) * 2 + core)
        act((x * ring + yy) * 2 + 1 - core)
        act((x * ring + yy) * 2 + core)
        return 0

    lax.fori_loop(0, ring - 1, one, 0)
    act(((1 - x) * ring + y) * 2 + 1 - core)
    act(((1 - x) * ring + y) * 2 + core)
    act((x * ring + y) * 2 + 1 - core)


def greet(n_node, n_feat):
    barrier = pltpu.get_barrier_semaphore()
    each_feat(n_feat, lambda p: pl.semaphore_signal(
        barrier, inc=1, device_id={"feat": p}, device_id_type=MESH))
    each_node(n_node, lambda p: pl.semaphore_signal(
        barrier, inc=1, device_id={"node": p}, device_id_type=MESH))
    return barrier, n_feat + n_node - 2


def push(src, dst, send_sem, recv_sem, where):
    pltpu.make_async_remote_copy(
        src_ref=src, dst_ref=dst, send_sem=send_sem, recv_sem=recv_sem,
        device_id=where, device_id_type=MESH,
    ).start()


def spread(axis, count, src_of, dst, send_sem, recv_sem):
    each = each_feat if axis == "feat" else each_node
    each(count, lambda p: push(src_of(p), dst, send_sem, recv_sem, {axis: p}))


def wait_bytes(view, sem):
    pltpu.make_async_copy(view, view, sem).wait()


def to_tile(rows):
    left = rows[:, :HALF]
    if rows.shape[1] < HALF:
        left = jnp.concatenate([rows, jnp.zeros((WIDTH, HALF - rows.shape[1]), F32)], axis=1)
    right = jnp.zeros((WIDTH, HALF), F32)
    if rows.shape[1] > HALF:
        over = rows[:, HALF:]
        right = jnp.concatenate([over, right[:, : 2 * HALF - rows.shape[1]]], axis=1)
    return jnp.concatenate([left, right], axis=0)


def from_tiles(tiles, width):
    tiles = tiles.astype(F32)
    return jnp.concatenate([tiles[:, :WIDTH], tiles[:, WIDTH:]], axis=2).reshape(-1, 2 * HALF)[:, :width]


class Ring:
    def __init__(self, size, view, target, near, far, sems, first, send_sem, landed):
        self.size, self.half, self.view, self.target = size, size // 2, view, target
        self.near, self.far, self.sems, self.ids, self.send_sem = near, far, sems, {}, send_sem
        self.first, self.landed, self.sent = first, landed, 0

    def sem(self, name):
        number = self.ids.setdefault(name, len(self.ids))
        return self.sems.at[self.first + number]

    def pieces(self, step, way):
        return self.near if step < self.half else self.far[way]

    def move(self, name, ref, where, count):
        push(ref, ref, self.send_sem, self.sem(name), where)
        self.sent += count

    def pass_on(self, step, way, side, lo, hi):
        if step >= self.half:
            return
        for s2, lo2, hi2 in self.pieces(step + 1, way):
            if s2 == side and lo2 >= lo and hi2 <= hi:
                self.move((way, step + 1, s2, lo2), self.view(side, -way * step, lo2, hi2),
                          self.target(way), hi2 - lo2)

    def receive(self, step):
        for pair in zip(self.pieces(step, 1), self.pieces(step, -1)):
            for way, (side, lo, hi) in zip((1, -1), pair):
                ref = self.view(side, -way * step, lo, hi)
                wait_bytes(ref, self.sem((way, step, side, lo)))
                self.pass_on(step, way, side, lo, hi)
                self.landed(way, step, side, lo, hi, ref)


def slot_table(n_node, n_feat, row, col, fill):
    me = lax.axis_index("node")
    slot = lax.broadcasted_iota(jnp.int32, (1, TILE), 1)
    shift = lax.rem(31 * (me * TILE + slot), MOD)
    low = jnp.where(shift == 0, 0, MOD - shift)
    bound = jnp.where(fill > 0, fill + jnp.where(low + fill > MOD, 256 - MOD, 0), 0)
    group = lax.div(col, n_feat)
    member = col - group * n_feat
    key = (jnp.where(fill > 0, group, n_node) * TILE + slot).astype(F32)
    keys = jnp.broadcast_to(key, (TILE, TILE))
    keys_t = keys.T
    rank = jnp.sum((keys_t < keys).astype(F32), axis=0, keepdims=True)
    place = lax.broadcasted_iota(jnp.int32, (TILE, TILE), 0).astype(F32)
    chosen = (place == rank).astype(F32).astype(BF16)
    line = lax.broadcasted_iota(jnp.int32, (8, TILE), 0)
    which = lax.rem(line, 4)
    payload = jnp.where(
        which == 0, low, jnp.where(which == 1, bound, jnp.where(which == 2, row, member))
    ).astype(F32).astype(BF16)
    ordered = lax.dot_general(
        payload, chosen, (((1,), (1,)), ((), ())), preferred_element_type=F32
    )
    head = jnp.where(line[:, :HALF] < 4, ordered[:, :HALF], ordered[:, HALF:])
    edge = (lax.broadcasted_iota(jnp.int32, (1, HALF), 1) * TILE).astype(F32)
    before = jnp.sum((keys_t[:, :HALF] < edge).astype(F32), axis=0, keepdims=True)
    return jnp.concatenate([head, jnp.broadcast_to(before, (8, HALF))], axis=0).astype(BF16)


def exchange_kernel(
    n_node, n_feat,
    feat_hbm, cot_hbm, deg_hbm, row_hbm, col_hbm, fill_hbm,
    blocks, feats, self_out,
    cot, ints, send, g_send, g_feat, g_node, g_tile, g_back,
    in_sems, a_sems, g_sems, y_sems, z_sems, end_sems,
):
    node_y, ring_z = n_node // 4, n_feat // 2
    span = n_feat + 1
    cut = (span * 11) // 25
    width = cot.shape[0]
    x, y, core = node_coords(node_y)
    me_n, me_f = lax.axis_index("node"), lax.axis_index("feat")
    hi, z = lax.div(me_f, ring_z), lax.rem(me_f, ring_z)
    loads = [
        pltpu.make_async_copy(src, dst, in_sems.at[k])
        for k, (src, dst) in enumerate((
            (cot_hbm, cot), (deg_hbm, ints.at[0]), (feat_hbm, feats.at[me_f]),
            (row_hbm, ints.at[1]), (col_hbm, ints.at[2]), (fill_hbm, ints.at[3]),
        ))
    ]
    for load in loads:
        load.start()
    barrier, expected = greet(n_node, n_feat)
    loads[0].wait()
    loads[1].wait()
    scaled = cot[...].astype(F32) / ints[0].astype(F32)
    for j in range(n_feat):
        part = scaled[j * WIDTH:(j + 1) * WIDTH]
        send[j] = jnp.concatenate([part[:, :HALF], part[:, HALF:]], axis=0).astype(BF16)
    home = me_n * span
    blocks[home + me_f] = send[me_f]
    for load in loads[2:]:
        load.wait()
    blocks[home + n_feat] = slot_table(n_node, n_feat, ints[1], ints[2], ints[3])
    pl.semaphore_wait(barrier, expected)

    spread("feat", n_feat, lambda p: send.at[p], blocks.at[home + me_f], a_sems.at[0], a_sems.at[1])

    def z_view(side, offset, lo, hi_row):
        hh = hi if side == 0 else 1 - hi
        return feats.at[hh * ring_z + wrap(z + offset, ring_z), pl.ds(lo, hi_row - lo)]

    mid = width // 2
    z_near = [(0, 0, mid), (0, mid, width), (1, 0, mid), (1, mid, width)]
    z_ring = Ring(
        ring_z, z_view, lambda way: {"feat": hi * ring_z + wrap(z + way, ring_z)},
        z_near, {1: z_near[:2], -1: z_near[2:]}, z_sems, 0, end_sems.at[3], lambda *_: None,
    )
    for side, lo, up in z_near[:2]:
        for way in (1, -1):
            z_ring.pass_on(0, way, side, lo, up)
        z_ring.move(("x", lo), z_view(0, 0, lo, up), {"feat": (1 - hi) * ring_z + z}, up - lo)

    local = lax.dot_general(
        feats[me_f], cot[...], (((1,), (1,)), ((), ())), preferred_element_type=F32
    )
    for j in range(n_feat):
        g_send[j] = to_tile(local[j * WIDTH:(j + 1) * WIDTH]).astype(BF16)
    g_feat[me_f] = g_send[me_f]
    spread("feat", n_feat, lambda p: g_send.at[p], g_feat.at[me_f], g_sems.at[0], g_sems.at[1])

    def z_partner():
        for side, lo, up in z_near[2:]:
            wait_bytes(z_view(1, 0, lo, up), z_ring.sem(("x", lo)))
            for way in (1, -1):
                z_ring.pass_on(0, way, 1, lo, up)

    z_partner()
    wait_bytes(send.at[pl.ds(0, n_feat - 1)], a_sems.at[1])

    def node_at(xx, yy, cc):
        return (xx * node_y + yy) * 2 + cc

    def y_view(side, offset, lo, up):
        xx = x if side == 0 else 1 - x
        return blocks.at[pl.ds(node_at(xx, wrap(y + offset, node_y), core) * span + lo, up - lo)]

    def to_sibling(ref):
        push(ref, ref, end_sems.at[1], end_sems.at[2], {"node": node_at(x, y, 1 - core)})

    fresh = []

    def y_landed(way, step, side, lo, up, ref):
        if side == 0 and lo >= cut:
            name = ("x", way, step, lo)
            y_ring.move(name, ref, partner, up - lo)
            fresh.append((name, -way * step, lo, up))
        to_sibling(ref)

    partner = {"node": node_at(1 - x, y, core)}
    room = (span + cut) // 2
    y_near = [(0, cut, span), (0, 0, cut), (1, 0, cut)]
    y_ring = Ring(
        node_y, y_view, lambda way: {"node": node_at(x, wrap(y + way, node_y), core)}, y_near,
        {1: [(0, cut, room), (0, 0, cut)], -1: [(0, room, span), (1, 0, cut)]},
        y_sems, 0, end_sems.at[0], y_landed,
    )

    def from_partner():
        waiting = list(fresh)
        fresh.clear()
        return waiting

    def drain(waiting):
        for name, offset, lo, up in waiting:
            ref = y_view(1, offset, lo, up)
            wait_bytes(ref, y_ring.sem(name))
            to_sibling(ref)

    for side, lo, up in ((0, 0, cut), (0, cut, span)):
        y_ring.move(("x", 0, 0, lo), y_view(0, 0, lo, up), partner, up - lo)
        for way in (1, -1):
            y_ring.pass_on(0, way, side, lo, up)
    to_sibling(y_view(0, 0, 0, span))
    fresh.append((("x", 0, 0, cut), 0, cut, span))

    z_ring.receive(1)
    ref = y_view(1, 0, 0, cut)
    wait_bytes(ref, y_ring.sem(("x", 0, 0, 0)))
    for way in (1, -1):
        y_ring.pass_on(0, way, 1, 0, cut)
    to_sibling(ref)
    wait_bytes(g_feat.at[pl.ds(0, n_feat - 1)], g_sems.at[1])
    g_tile[...] = jnp.sum(g_feat[...].astype(F32), axis=0)
    g_node[me_n] = g_tile[...]
    spread("node", n_node, lambda p: g_tile, g_node.at[me_n], g_sems.at[2], g_sems.at[3])

    waiting = from_partner()
    z_step = 1
    for step in range(1, node_y // 2 + 1):
        y_ring.receive(step)
        drain(waiting)
        waiting = from_partner()
        if z_step < ring_z // 2:
            z_step += 1
            z_ring.receive(z_step)
        if step == 1:
            wait_bytes(g_node.at[pl.ds(0, n_node - 1)], g_sems.at[3])
            g_back[me_f] = jnp.sum(g_node[...], axis=0).astype(BF16)
            spread("feat", n_feat, lambda p: g_back.at[me_f], g_back.at[me_f], g_sems.at[4], g_sems.at[5])
    drain(waiting)
    while z_step < ring_z // 2:
        z_step += 1
        z_ring.receive(z_step)

    wait_bytes(g_back.at[pl.ds(0, n_feat - 1)], g_sems.at[5])
    self_out[...] = from_tiles(g_back[...], width) * (1.0 / math.sqrt(n_node * n_feat * TILE))
    wait_bytes(send.at[pl.ds(0, n_feat - 1)], a_sems.at[0])
    wait_bytes(g_send.at[pl.ds(0, n_feat - 1)], g_sems.at[0])
    wait_bytes(g_node.at[pl.ds(0, n_node - 1)], g_sems.at[2])
    wait_bytes(g_back.at[pl.ds(0, n_feat - 1)], g_sems.at[4])
    wait_bytes(blocks.at[pl.ds(0, n_node // 2 * span)], end_sems.at[2])
    wait_bytes(blocks.at[pl.ds(0, n_node // 2 * span)], end_sems.at[1])
    wait_bytes(blocks.at[pl.ds(0, y_ring.sent)], end_sems.at[0])
    wait_bytes(feats.at[pl.ds(0, z_ring.sent // width)], end_sems.at[3])


def slots_kernel(
    n_node, n_feat, blocks, feats, out, neigh_out,
    acc, base, packed, before, packed_s, before_s, todo, sems,
):
    span = n_feat + 1
    me = lax.axis_index("node")

    table = blocks[...].reshape(n_node, span, 16, HALF)[:, n_feat].astype(F32).astype(jnp.int32)
    for k in range(2):
        low = table[:, 4 * k, :]
        bound = table[:, 4 * k + 1, :]
        row = table[:, 4 * k + 2, :]
        member = table[:, 4 * k + 3, :]
        first = lax.broadcasted_iota(jnp.int32, (n_node, HALF), 0) * span
        packed[k] = (first + row) + low * 1024 + bound * (1 << 18) + member * (1 << 25)
    before[...] = table[:, 8, :]
    moves = [
        pltpu.make_async_copy(packed, packed_s, sems.at[0]),
        pltpu.make_async_copy(before, before_s, sems.at[1]),
    ]
    for one in moves:
        one.start()

    r = lax.broadcasted_iota(jnp.int32, (TILE, TILE), 0)
    c = lax.broadcasted_iota(jnp.int32, (TILE, TILE), 1)
    residue = lax.rem(13 * r * r + 7 * r * c + 197 * c, MOD)
    base[...] = (residue * 256 - 32768).astype(jnp.int16)
    acc[...] = jnp.zeros_like(acc)
    for one in moves:
        one.wait()

    def collect_group(g, count):
        start, stop = before_s[g, me], before_s[g, me + 1]

        def put(i, at):
            todo[at] = packed_s[lax.div(i, HALF), g, lax.rem(i, HALF)]
            return at + 1

        return lax.fori_loop(start, stop, put, count)

    count = lax.fori_loop(0, n_node, collect_group, 0)
    for k in range(UNROLL - 1):
        todo[count + k] = 0

    def turn(i, _):
        sums = []
        for k in range(UNROLL):
            entry = todo[i * UNROLL + k]
            place = jnp.bitwise_and(entry, 1023)
            low = jnp.bitwise_and(lax.shift_right_logical(entry, 10), 255)
            bound = jnp.bitwise_and(lax.shift_right_logical(entry, 18), 127)
            pair = blocks[place].astype(F32)
            source = jnp.concatenate([pair[:8], pair[8:]], axis=1).astype(BF16)
            moved = base[...] - jnp.full((TILE, TILE), low * 256, jnp.int32).astype(jnp.int16)
            limit = jnp.full((TILE, TILE), bound * 256 - 32768, jnp.int32).astype(jnp.int16)
            pattern = jnp.where(moved < limit, jnp.ones((), BF16), jnp.zeros((), BF16))
            sums.append((lax.shift_right_logical(entry, 25),
                         jnp.dot(source, pattern, preferred_element_type=F32)))
        for member, product in sums:
            acc[member] += product
        return 0

    lax.fori_loop(0, lax.div(count + UNROLL - 1, UNROLL), turn, 0)
    total = jnp.zeros((WIDTH, feats.shape[1]), F32)
    for m in range(n_feat):
        part = acc[m]
        out[m] = jnp.concatenate([part[:, :HALF], part[:, HALF:]], axis=0).astype(BF16)
        total += lax.dot_general(
            part.astype(BF16), feats[m], (((1,), (1,)), ((), ())), preferred_element_type=F32
        )
    neigh_out[...] = to_tile(total).astype(BF16)


def finish_kernel(
    n_node, n_feat,
    slices, neigh, cot, w_self, w_neigh,
    grad_out, neigh_out,
    landed, g_node, g_back, g_sems, a_sems,
):
    width = cot.shape[0]
    me_n, me_f = lax.axis_index("node"), lax.axis_index("feat")
    barrier, expected = greet(n_node, n_feat)
    landed[me_f] = slices[me_f]
    g_node[me_n] = neigh[...]
    own = jnp.dot(w_self[...], cot[...], preferred_element_type=F32)
    pl.semaphore_wait(barrier, expected)
    spread("node", n_node, lambda p: neigh, g_node.at[me_n], g_sems.at[0], g_sems.at[1])
    spread("feat", n_feat, lambda p: slices.at[p], landed.at[me_f], a_sems.at[0], a_sems.at[1])
    wait_bytes(g_node.at[pl.ds(0, n_node - 1)], g_sems.at[1])
    g_back[me_f] = jnp.sum(g_node[...].astype(F32), axis=0).astype(BF16)
    spread("feat", n_feat, lambda p: g_back.at[me_f], g_back.at[me_f], g_sems.at[2], g_sems.at[3])
    wait_bytes(landed.at[pl.ds(0, n_feat - 1)], a_sems.at[1])
    gathered = from_tiles(landed[...], TILE).astype(BF16)
    grad_out[...] = (
        own + jnp.dot(w_neigh[...], gathered, preferred_element_type=F32)
    ).astype(BF16)
    wait_bytes(g_back.at[pl.ds(0, n_feat - 1)], g_sems.at[3])
    neigh_out[...] = from_tiles(g_back[...], width).T * (1.0 / math.sqrt(n_node * n_feat * TILE))
    wait_bytes(g_back.at[pl.ds(0, n_feat - 1)], g_sems.at[2])
    wait_bytes(g_node.at[pl.ds(0, n_node - 1)], g_sems.at[0])
    wait_bytes(slices.at[pl.ds(0, n_feat - 1)], a_sems.at[0])


def in_vmem(count):
    return [pl.BlockSpec(memory_space=pltpu.VMEM)] * count


def local(n_node, n_feat, features, cotangent, w_self, w_neigh, degree, tile_row, tile_col, tile_fill):
    width = n_feat * WIDTH
    span = n_feat + 1
    line = (1, TILE)
    tile = (16, HALF)
    shape = jax.ShapeDtypeStruct
    dma = pltpu.SemaphoreType.DMA
    cot_t = cotangent.T
    blocks, feats, self_grad = pl.pallas_call(
        functools.partial(exchange_kernel, n_node, n_feat),
        out_shape=(
            shape((n_node * span, *tile), BF16),
            shape((n_feat, width, TILE), BF16),
            shape((width, width), F32),
        ),
        in_specs=[pl.BlockSpec(memory_space=pltpu.HBM)] * 6,
        out_specs=tuple(in_vmem(3)),
        scratch_shapes=[
            pltpu.VMEM((width, TILE), BF16),
            pltpu.VMEM((4, *line), jnp.int32),
            pltpu.VMEM((n_feat, *tile), BF16),
            pltpu.VMEM((n_feat, *tile), BF16),
            pltpu.VMEM((n_feat, *tile), BF16),
            pltpu.VMEM((n_node, *tile), F32),
            pltpu.VMEM(tile, F32),
            pltpu.VMEM((n_feat, *tile), BF16),
            dma((6,)), dma((2,)), dma((6,)), dma((64,)), dma((64,)), dma((4,)),
        ],
        compiler_params=pltpu.CompilerParams(
            collective_id=0, has_side_effects=True, vmem_limit_bytes=32 << 20
        ),
        name="exchange",
    )(
        features.T, cot_t, degree.reshape(line), tile_row.reshape(line),
        tile_col.reshape(line), tile_fill.reshape(line),
    )
    slices, neigh = pl.pallas_call(
        functools.partial(slots_kernel, n_node, n_feat),
        out_shape=(shape((n_feat, *tile), BF16), shape(tile, BF16)),
        in_specs=in_vmem(2),
        out_specs=tuple(in_vmem(2)),
        scratch_shapes=[
            pltpu.VMEM((n_feat, WIDTH, TILE), F32),
            pltpu.VMEM((TILE, TILE), jnp.int16),
            pltpu.VMEM((2, n_node, HALF), jnp.int32),
            pltpu.VMEM((n_node, HALF), jnp.int32),
            pltpu.SMEM((2, n_node, HALF), jnp.int32),
            pltpu.SMEM((n_node, HALF), jnp.int32),
            pltpu.SMEM((n_node * TILE + UNROLL,), jnp.int32),
            dma((2,)),
        ],
        compiler_params=pltpu.CompilerParams(vmem_limit_bytes=32 << 20),
        name="slots",
    )(blocks, feats)
    input_grad, neigh_grad = pl.pallas_call(
        functools.partial(finish_kernel, n_node, n_feat),
        out_shape=(shape((width, TILE), BF16), shape((width, width), F32)),
        in_specs=in_vmem(5),
        out_specs=tuple(in_vmem(2)),
        scratch_shapes=[
            pltpu.VMEM((n_feat, *tile), BF16),
            pltpu.VMEM((n_node, *tile), BF16),
            pltpu.VMEM((n_feat, *tile), BF16),
            dma((4,)), dma((2,)),
        ],
        compiler_params=pltpu.CompilerParams(
            collective_id=1, has_side_effects=True, vmem_limit_bytes=32 << 20
        ),
        name="finish",
    )(slices, neigh, cot_t, w_self, w_neigh)
    return input_grad.T, self_grad, neigh_grad


def solution(mesh):
    n_node, n_feat = mesh.shape["node"], mesh.shape["feat"]
    return jax.shard_map(
        functools.partial(local, n_node, n_feat),
        mesh=mesh,
        in_specs=(
            P(("node", "feat"), None),
            P(("node", "feat"), None),
            P(),
            P(),
            P(("node", "feat")),
            P("node"),
            P("node"),
            P("node"),
        ),
        out_specs=(P(("node", "feat"), None), P(), P()),
        check_vma=False,
    )
```

```python
import functools
import math

import jax
import jax.numpy as jnp
from jax import lax
from jax.experimental import pallas as pl
from jax.experimental.pallas import tpu as pltpu
from jax.sharding import PartitionSpec as P

TILE = 256
HALF = TILE // 2
WIDTH = 8
MOD = 251
UNROLL = 16
ROOM = 256
MESH = pl.DeviceIdType.MESH
F32 = jnp.float32
BF16 = jnp.bfloat16


def node_coords(node_y):
    me = lax.axis_index("node")
    core = lax.rem(me, 2)
    y = lax.rem(lax.div(me, 2), node_y)
    x = lax.div(me, 2 * node_y)
    return x, y, core


def wrap(value, size):
    return lax.rem(value + size, size)


def far_step(t, size):
    back = lax.div(t + 1, 2)
    return lax.rem(size // 2 + jnp.where(lax.rem(t, 2) == 1, size - back, back), size)


def each_feat(n_feat, act):
    ring = n_feat // 2
    me = lax.axis_index("feat")
    hi, z = lax.div(me, ring), lax.rem(me, ring)

    def one(t, _):
        zz = lax.rem(z + far_step(t, ring), ring)
        act((1 - hi) * ring + zz)
        act(hi * ring + zz)
        return 0

    lax.fori_loop(0, ring - 1, one, 0)
    act((1 - hi) * ring + z)


def each_node(n_node, act):
    ring = n_node // 4
    x, y, core = node_coords(ring)

    def one(t, _):
        yy = lax.rem(y + far_step(t, ring), ring)
        act(((1 - x) * ring + yy) * 2 + 1 - core)
        act(((1 - x) * ring + yy) * 2 + core)
        act((x * ring + yy) * 2 + 1 - core)
        act((x * ring + yy) * 2 + core)
        return 0

    lax.fori_loop(0, ring - 1, one, 0)
    act(((1 - x) * ring + y) * 2 + 1 - core)
    act(((1 - x) * ring + y) * 2 + core)
    act((x * ring + y) * 2 + 1 - core)


def greet(n_node, n_feat):
    barrier = pltpu.get_barrier_semaphore()
    each_feat(n_feat, lambda p: pl.semaphore_signal(
        barrier, inc=1, device_id={"feat": p}, device_id_type=MESH))
    each_node(n_node, lambda p: pl.semaphore_signal(
        barrier, inc=1, device_id={"node": p}, device_id_type=MESH))
    return barrier, n_feat + n_node - 2


def push(src, dst, send_sem, recv_sem, where):
    pltpu.make_async_remote_copy(
        src_ref=src, dst_ref=dst, send_sem=send_sem, recv_sem=recv_sem,
        device_id=where, device_id_type=MESH,
    ).start()


def spread(axis, count, src_of, dst, send_sem, recv_sem):
    each = each_feat if axis == "feat" else each_node
    each(count, lambda p: push(src_of(p), dst, send_sem, recv_sem, {axis: p}))


def wait_bytes(view, sem):
    pltpu.make_async_copy(view, view, sem).wait()


def to_tile(rows):
    left = rows[:, :HALF]
    if rows.shape[1] < HALF:
        left = jnp.concatenate([rows, jnp.zeros((WIDTH, HALF - rows.shape[1]), F32)], axis=1)
    right = jnp.zeros((WIDTH, HALF), F32)
    if rows.shape[1] > HALF:
        over = rows[:, HALF:]
        right = jnp.concatenate([over, right[:, : 2 * HALF - rows.shape[1]]], axis=1)
    return jnp.concatenate([left, right], axis=0)


def from_tiles(tiles, width):
    tiles = tiles.astype(F32)
    return jnp.concatenate([tiles[:, :WIDTH], tiles[:, WIDTH:]], axis=2).reshape(-1, 2 * HALF)[:, :width]


class Ring:
    def __init__(self, size, view, target, near, far, sems, first, send_sem, landed):
        self.size, self.half, self.view, self.target = size, size // 2, view, target
        self.near, self.far, self.sems, self.ids, self.send_sem = near, far, sems, {}, send_sem
        self.first, self.landed, self.sent = first, landed, 0

    def sem(self, name):
        number = self.ids.setdefault(name, len(self.ids))
        return self.sems.at[self.first + number]

    def pieces(self, step, way):
        return self.near if step < self.half else self.far[way]

    def move(self, name, ref, where, count):
        push(ref, ref, self.send_sem, self.sem(name), where)
        self.sent += count

    def pass_on(self, step, way, side, lo, hi):
        if step >= self.half:
            return
        for s2, lo2, hi2 in self.pieces(step + 1, way):
            if s2 == side and lo2 >= lo and hi2 <= hi:
                self.move((way, step + 1, s2, lo2), self.view(side, -way * step, lo2, hi2),
                          self.target(way), hi2 - lo2)

    def receive(self, step):
        for pair in zip(self.pieces(step, 1), self.pieces(step, -1)):
            for way, (side, lo, hi) in zip((1, -1), pair):
                ref = self.view(side, -way * step, lo, hi)
                wait_bytes(ref, self.sem((way, step, side, lo)))
                self.pass_on(step, way, side, lo, hi)
                self.landed(way, step, side, lo, hi, ref)


def ranks(key):
    keys = jnp.broadcast_to(key, (TILE, TILE))
    keys_t = keys.T
    rank = jnp.sum((keys_t < keys).astype(F32), axis=0, keepdims=True)
    place = lax.broadcasted_iota(jnp.int32, (TILE, TILE), 0).astype(F32)
    return (place == rank).astype(F32).astype(BF16), keys_t


def count_below(keys_t, first):
    edge = ((lax.broadcasted_iota(jnp.int32, (1, HALF), 1) + first) * TILE).astype(F32)
    return jnp.sum((keys_t[:, :HALF] < edge).astype(F32), axis=0, keepdims=True)


def slot_table(n_node, n_feat, row, col, fill):
    me = lax.axis_index("node")
    ring_y = n_node // 8
    slot = lax.broadcasted_iota(jnp.int32, (1, TILE), 1)
    shift = lax.rem(31 * (me * TILE + slot), MOD)
    low = jnp.where(shift == 0, 0, MOD - shift)
    bound = jnp.where(fill > 0, fill + jnp.where(low + fill > MOD, 256 - MOD, 0), 0)
    group = lax.div(col, n_feat)
    far = lax.div(group, 4 * ring_y)
    in_line = group - far * (4 * ring_y)
    quad = lax.div(in_line, 4)
    rest = in_line - quad * 4
    y_lo = lax.div(rest, 2)
    core = rest - y_lo * 2
    side = far * 2 + y_lo
    member = side * n_feat + col - group * n_feat
    order = (quad * 2 + core) * 4 + side
    key = (jnp.where(fill > 0, order, n_node) * TILE + slot).astype(F32)
    chosen, keys_t = ranks(key)
    line = lax.broadcasted_iota(jnp.int32, (8, TILE), 0)
    which = lax.rem(line, 4)
    payload = jnp.where(
        which == 0, low, jnp.where(which == 1, bound, jnp.where(which == 2, row, member))
    ).astype(F32).astype(BF16)
    ordered = lax.dot_general(
        payload, chosen, (((1,), (1,)), ((), ())), preferred_element_type=F32
    )
    head = jnp.where(line[:, :HALF] < 4, ordered[:, :HALF], ordered[:, HALF:])
    before = count_below(keys_t, 0)
    return jnp.concatenate([head, jnp.broadcast_to(before, (8, HALF))], axis=0).astype(BF16)


def own_slots(sources, span, mine, members, tables):
    i_at = lax.broadcasted_iota(jnp.int32, (TILE, TILE), 0).astype(F32)
    p_at = lax.broadcasted_iota(jnp.int32, (TILE, TILE), 1).astype(F32)
    apart = i_at - p_at
    lane = lax.broadcasted_iota(jnp.int32, (1, HALF), 1)
    line = lax.broadcasted_iota(jnp.int32, (8, TILE), 0)
    total = jnp.zeros((1, 1), F32)
    found = jnp.zeros((8, TILE), F32)
    for s in range(sources):
        table = tables(s).astype(F32)
        top, before = table[:8], table[8:9]
        payload = jnp.concatenate([top, jnp.concatenate([top[4:], top[:4]], axis=0)], axis=1)
        payload = payload + jnp.where(line == 2, float(s * span), 0.0)
        begin = jnp.sum(jnp.where(lane == 4 * mine, before, 0.0), axis=1, keepdims=True)
        end = jnp.sum(jnp.where(lane == 4 * mine + 4, before, 0.0), axis=1, keepdims=True)
        here = (apart == begin - total) & (i_at >= begin) & (i_at < end)
        found += jnp.dot(
            payload.astype(BF16), here.astype(F32).astype(BF16), preferred_element_type=F32
        )
        total += end - begin
    place = lax.broadcasted_iota(jnp.int32, (1, TILE), 1).astype(F32)
    key = jnp.where(place < total, found[3:4], float(members)) * TILE + place
    chosen, keys_t = ranks(key)
    ordered = lax.dot_general(
        found.astype(BF16), chosen, (((1,), (1,)), ((), ())), preferred_element_type=F32
    ).astype(jnp.int32)
    packed = (
        ordered[0:1] + ordered[1:2] * (1 << 8) + ordered[2:3] * (1 << 16) + ordered[3:4] * (1 << 24)
    )
    upto = count_below(keys_t, 1).astype(jnp.int32)
    upto = jnp.concatenate([upto, upto], axis=1)
    return jnp.where(line == 0, packed, upto), (total > float(ROOM)).astype(F32)


def layer_kernel(
    n_node, n_feat,
    feat_hbm, cot_hbm, ints, w_self, w_neigh,
    grad_out, self_out, neigh_out, flag_out,
    blocks, feats, feat, cot, send, g_send, g_feat, g_node, g_tile, s_back,
    base, todo, todo_s, sums, partial, parts, slices, landed, paired, n_send, n_node_sum, n_back,
    in_sems, a_sems, g_sems, y_sems, z_sems, end_sems, c_sems,
):
    ring_y, ring_z = n_node // 8, n_feat // 2
    sources, span = 2 * ring_y, n_feat + 1
    width = cot.shape[0]
    factor = 1.0 / math.sqrt(n_node * n_feat * TILE)
    x, y, core = node_coords(2 * ring_y)
    y_hi, y_lo = lax.div(y, 2), lax.rem(y, 2)
    me_n, me_f = lax.axis_index("node"), lax.axis_index("feat")
    hi, z = lax.div(me_f, ring_z), lax.rem(me_f, ring_z)
    mine = x * 2 + y_lo
    loads = [
        pltpu.make_async_copy(cot_hbm, cot, in_sems.at[0]),
        pltpu.make_async_copy(feat_hbm, feat, in_sems.at[1]),
    ]
    for load in loads:
        load.start()
    barrier, expected = greet(n_node, n_feat)
    loads[0].wait()
    scaled = cot[...].astype(F32) / ints[0].astype(F32)
    for j in range(n_feat):
        part = scaled[j * WIDTH:(j + 1) * WIDTH]
        send[j] = jnp.concatenate([part[:, :HALF], part[:, HALF:]], axis=0).astype(BF16)
    home = (y_hi * 2 + core) * span
    blocks[home + me_f] = send[me_f]
    loads[1].wait()
    wide = width // 2
    feats[me_f] = feat[pl.ds(pl.multiple_of(hi * wide, 16), wide)]
    pl.semaphore_wait(barrier, expected)

    spread("feat", n_feat, lambda p: send.at[p], blocks.at[home + me_f], a_sems.at[0], a_sems.at[1])

    def z_view(side, offset, lo, up):
        hh = hi if side == 0 else 1 - hi
        return feats.at[hh * ring_z + wrap(z + offset, ring_z), pl.ds(lo, up - lo)]

    z_near = [(0, 0, wide), (1, 0, wide)]
    z_ring = Ring(
        ring_z, z_view, lambda way: {"feat": hi * ring_z + wrap(z + way, ring_z)},
        z_near, {1: z_near[:1], -1: z_near[1:]}, z_sems, 0, end_sems.at[3], lambda *_: None,
    )
    x_partner = {"feat": (1 - hi) * ring_z + z}
    push(feat.at[pl.ds(pl.multiple_of((1 - hi) * wide, 16), wide)], feats.at[me_f],
         end_sems.at[3], z_ring.sem("x"), x_partner)
    for way in (1, -1):
        z_ring.pass_on(0, way, 0, 0, wide)

    blocks[home + n_feat] = slot_table(n_node, n_feat, ints[1], ints[2], ints[3])
    local = lax.dot_general(
        feat[...], cot[...], (((1,), (1,)), ((), ())), preferred_element_type=F32
    )
    for j in range(n_feat):
        g_send[j] = to_tile(local[j * WIDTH:(j + 1) * WIDTH]).astype(BF16)
    g_feat[me_f] = g_send[me_f]
    spread("feat", n_feat, lambda p: g_send.at[p], g_feat.at[me_f], g_sems.at[0], g_sems.at[1])
    wait_bytes(z_view(1, 0, 0, wide), z_ring.sem("x"))
    for way in (1, -1):
        z_ring.pass_on(0, way, 1, 0, wide)
    z_step = [0]

    def z_turn():
        if z_step[0] < ring_z // 2:
            z_step[0] += 1
            z_ring.receive(z_step[0])

    wait_bytes(send.at[pl.ds(0, n_feat - 1)], a_sems.at[1])

    def node_at(xx, yy, cc):
        return (xx * 2 * ring_y + yy) * 2 + cc

    def y_view(side, offset, lo, up):
        return blocks.at[pl.ds((wrap(y_hi + offset, ring_y) * 2 + core) * span + lo, up - lo)]

    def to_sibling(ref):
        push(ref, ref, end_sems.at[1], end_sems.at[2], {"node": node_at(x, y, 1 - core)})

    cut = span // 2
    y_near = [(0, 0, cut), (0, cut, span)]
    y_ring = Ring(
        ring_y, y_view,
        lambda way: {"node": node_at(x, wrap(y_hi + way, ring_y) * 2 + y_lo, core)},
        y_near, {1: y_near[:1], -1: y_near[1:]}, y_sems, 0, end_sems.at[0],
        lambda way, step, side, lo, up, ref: to_sibling(ref),
    )
    for side, lo, up in y_near:
        for way in (1, -1):
            y_ring.pass_on(0, way, side, lo, up)
    to_sibling(y_view(0, 0, 0, span))

    z_turn()
    wait_bytes(g_feat.at[pl.ds(0, n_feat - 1)], g_sems.at[1])
    g_tile[...] = jnp.sum(g_feat[...].astype(F32), axis=0).astype(BF16)
    g_node[me_n] = g_tile[...]
    spread("node", n_node, lambda p: g_tile, g_node.at[me_n], g_sems.at[2], g_sems.at[3])

    r = lax.broadcasted_iota(jnp.int32, (TILE, TILE), 0)
    c = lax.broadcasted_iota(jnp.int32, (TILE, TILE), 1)
    residue = lax.rem(13 * r * r + 7 * r * c + 197 * c, MOD)
    base[...] = (residue * 256 - 32768).astype(jnp.int16)
    own = jnp.dot(w_self[...], cot[...], preferred_element_type=F32)

    for step in range(1, ring_y // 2 + 1):
        y_ring.receive(step)
        z_turn()
    wait_bytes(blocks.at[pl.ds(0, ring_y * span)], end_sems.at[2])
    listed, over = own_slots(
        sources, span, y_hi * 2 + core, 4 * n_feat, lambda s: blocks[s * span + n_feat]
    )
    todo[...] = listed
    to_scalars = pltpu.make_async_copy(todo, todo_s, in_sems.at[0])
    to_scalars.start()
    wait_bytes(g_node.at[pl.ds(0, n_node - 1)], g_sems.at[3])
    s_back[me_f] = jnp.sum(g_node[...].astype(F32), axis=0).astype(BF16)
    spread("feat", n_feat, lambda p: s_back.at[me_f], s_back.at[me_f], g_sems.at[4], g_sems.at[5])
    to_scalars.wait()
    z_turn()

    def turn(i, running):
        products = []
        for k in range(UNROLL):
            at = i * UNROLL + k
            entry = todo_s[0, at]
            member = lax.shift_right_logical(entry, 24)
            last = lax.shift_right_logical(todo_s[0, jnp.maximum(at - 1, 0)], 24)
            low = jnp.bitwise_and(entry, 255)
            bound = jnp.bitwise_and(lax.shift_right_logical(entry, 8), 255)
            place = jnp.bitwise_and(lax.shift_right_logical(entry, 16), 255)
            pair = blocks[jnp.minimum(place, sources * span - 1)].astype(F32)
            source = jnp.concatenate([pair[:8], pair[8:]], axis=1).astype(BF16)
            moved = base[...] - jnp.full((TILE, TILE), low * 256, jnp.int32).astype(jnp.int16)
            limit = jnp.full((TILE, TILE), bound * 256 - 32768, jnp.int32).astype(jnp.int16)
            pattern = jnp.where(moved < limit, jnp.ones((), BF16), jnp.zeros((), BF16))
            products.append((at, jnp.where(member == last, 1.0, 0.0),
                             jnp.dot(source, pattern, preferred_element_type=F32)))
        for at, keep, product in products:
            running = running * keep + product
            sums[at] = running
        return running

    running = jnp.zeros((WIDTH, TILE), F32)
    turns = ROOM // UNROLL
    quarter = turns // 4
    for part in range(4):
        running = lax.fori_loop(part * quarter, (part + 1) * quarter, turn, running)
        if part % 2 == 0:
            z_turn()
    for m in range(4 * n_feat):
        upto = todo_s[1, m]
        under = todo_s[1, m - 1] if m else 0
        part = sums[jnp.clip(upto - 1, 0, ROOM - 1)] * jnp.where(upto > under, 1.0, 0.0)
        partial[m // n_feat, m % n_feat] = jnp.concatenate(
            [part[:, :HALF], part[:, HALF:]], axis=0
        ).astype(BF16)

    parts[mine] = partial[mine]
    for dx, dy in ((1, 1), (0, 1), (1, 0)):
        xx, yy = wrap(x + dx, 2), wrap(y_lo + dy, 2)
        push(partial.at[xx * 2 + yy], parts.at[mine], c_sems.at[0], c_sems.at[1],
             {"node": node_at(xx, y_hi * 2 + yy, core)})
    while z_step[0] < ring_z // 2:
        z_turn()
    wait_bytes(parts.at[pl.ds(0, 3)], c_sems.at[1])
    total = parts[0].astype(F32)
    for k in range(1, 4):
        total += parts[k].astype(F32)
    slices[...] = total.astype(BF16)
    push(slices, paired, c_sems.at[8], c_sems.at[9], x_partner)
    landed[me_f] = slices[me_f]
    wait_bytes(paired, c_sems.at[9])
    grad = jnp.zeros((2 * WIDTH, wide), F32)
    for m in range(n_feat):
        rows = []
        for ref in (slices, paired):
            part = ref[m].astype(F32)
            rows.append(jnp.concatenate([part[:WIDTH], part[WIDTH:]], axis=1))
        grad += lax.dot_general(
            jnp.concatenate(rows, axis=0).astype(BF16), feats[m],
            (((1,), (1,)), ((), ())), preferred_element_type=F32,
        )
    swapped = jnp.concatenate([grad[WIDTH:], grad[:WIDTH]], axis=0)
    grad = jnp.where(hi == 0, grad, swapped)
    n_send[...] = jnp.concatenate(
        [grad, jnp.broadcast_to(over, (2 * WIDTH, HALF - wide))], axis=1
    ).astype(BF16)
    n_node_sum[me_n] = n_send[...]
    spread("node", n_node, lambda p: n_send, n_node_sum.at[me_n], c_sems.at[2], c_sems.at[3])
    spread("feat", n_feat, lambda p: slices.at[p], landed.at[me_f], c_sems.at[4], c_sems.at[5])
    wait_bytes(s_back.at[pl.ds(0, n_feat - 1)], g_sems.at[5])
    self_out[...] = from_tiles(s_back[...], width) * factor
    wait_bytes(n_node_sum.at[pl.ds(0, n_node - 1)], c_sems.at[3])
    n_back[me_f] = jnp.sum(n_node_sum[...].astype(F32), axis=0).astype(BF16)
    spread("feat", n_feat, lambda p: n_back.at[me_f], n_back.at[me_f], c_sems.at[6], c_sems.at[7])
    wait_bytes(landed.at[pl.ds(0, n_feat - 1)], c_sems.at[5])
    gathered = from_tiles(landed[...], TILE).astype(BF16)
    grad_out[...] = (
        own + jnp.dot(w_neigh[...], gathered, preferred_element_type=F32)
    ).astype(BF16)
    wait_bytes(send.at[pl.ds(0, n_feat - 1)], a_sems.at[0])
    wait_bytes(g_send.at[pl.ds(0, n_feat - 1)], g_sems.at[0])
    wait_bytes(g_node.at[pl.ds(0, n_node - 1)], g_sems.at[2])
    wait_bytes(s_back.at[pl.ds(0, n_feat - 1)], g_sems.at[4])
    wait_bytes(blocks.at[pl.ds(0, ring_y * span)], end_sems.at[1])
    wait_bytes(blocks.at[pl.ds(0, y_ring.sent)], end_sems.at[0])
    wait_bytes(feats.at[pl.ds(0, z_ring.sent // wide + 1)], end_sems.at[3])
    wait_bytes(parts.at[pl.ds(0, 3)], c_sems.at[0])
    wait_bytes(n_node_sum.at[pl.ds(0, n_node - 1)], c_sems.at[2])
    wait_bytes(landed.at[pl.ds(0, n_feat - 1)], c_sems.at[4])
    wait_bytes(n_back.at[pl.ds(0, n_feat - 1)], c_sems.at[7])
    wait_bytes(paired, c_sems.at[8])
    back = n_back[...].astype(F32)
    lines = []
    for half in range(2):
        part = back[:, half * WIDTH:(half + 1) * WIDTH, :wide].reshape(2, ring_z * WIDTH, wide)
        lines.append(jnp.concatenate([part[0], part[1]], axis=1))
    neigh_out[...] = jnp.concatenate(lines, axis=0).T * factor
    flag_out[...] = jnp.max(back, axis=0)[:, wide:]
    wait_bytes(n_back.at[pl.ds(0, n_feat - 1)], c_sems.at[6])


def in_vmem(count):
    return [pl.BlockSpec(memory_space=pltpu.VMEM)] * count


def few_slots(n_node, n_feat, features, cotangent, w_self, w_neigh, degree, tile_row, tile_col, tile_fill):
    width = n_feat * WIDTH
    span = n_feat + 1
    ring_y = n_node // 8
    tile = (16, HALF)
    shape = jax.ShapeDtypeStruct
    dma = pltpu.SemaphoreType.DMA
    vmem = pltpu.VMEM
    ints = jnp.stack([degree, tile_row, tile_col, tile_fill]).reshape(4, 1, TILE)
    input_grad, self_grad, neigh_grad, flag = pl.pallas_call(
        functools.partial(layer_kernel, n_node, n_feat),
        out_shape=(
            shape((width, TILE), BF16), shape((width, width), F32), shape((width, width), F32),
            shape((2 * WIDTH, HALF - width // 2), F32),
        ),
        in_specs=[pl.BlockSpec(memory_space=pltpu.HBM)] * 2 + in_vmem(3),
        out_specs=tuple(in_vmem(4)),
        scratch_shapes=[
            vmem((2 * ring_y * span, *tile), BF16),
            vmem((n_feat, width // 2, TILE), BF16),
            vmem((width, TILE), BF16),
            vmem((width, TILE), BF16),
            vmem((n_feat, *tile), BF16),
            vmem((n_feat, *tile), BF16),
            vmem((n_feat, *tile), BF16),
            vmem((n_node, *tile), BF16),
            vmem(tile, BF16),
            vmem((n_feat, *tile), BF16),
            vmem((TILE, TILE), jnp.int16),
            vmem((8, TILE), jnp.int32),
            pltpu.SMEM((8, TILE), jnp.int32),
            vmem((ROOM, WIDTH, TILE), F32),
            vmem((4, n_feat, *tile), BF16),
            vmem((4, n_feat, *tile), BF16),
            vmem((n_feat, *tile), BF16),
            vmem((n_feat, *tile), BF16),
            vmem((n_feat, *tile), BF16),
            vmem(tile, BF16),
            vmem((n_node, *tile), BF16),
            vmem((n_feat, *tile), BF16),
            dma((2,)), dma((2,)), dma((6,)), dma((16,)), dma((64,)), dma((4,)), dma((10,)),
        ],
        compiler_params=pltpu.CompilerParams(
            collective_id=0, has_side_effects=True, vmem_limit_bytes=40 << 20
        ),
        name="layer",
    )(features.T, cotangent.T, ints, w_self, w_neigh)
    return (input_grad.T, self_grad, neigh_grad), flag[0, 0]


def group_table(n_node, n_feat, row, col, fill):
    me = lax.axis_index("node")
    slot = lax.broadcasted_iota(jnp.int32, (1, TILE), 1)
    shift = lax.rem(31 * (me * TILE + slot), MOD)
    low = jnp.where(shift == 0, 0, MOD - shift)
    bound = jnp.where(fill > 0, fill + jnp.where(low + fill > MOD, 256 - MOD, 0), 0)
    group = lax.div(col, n_feat)
    member = col - group * n_feat
    key = (jnp.where(fill > 0, group, n_node) * TILE + slot).astype(F32)
    keys = jnp.broadcast_to(key, (TILE, TILE))
    keys_t = keys.T
    rank = jnp.sum((keys_t < keys).astype(F32), axis=0, keepdims=True)
    place = lax.broadcasted_iota(jnp.int32, (TILE, TILE), 0).astype(F32)
    chosen = (place == rank).astype(F32).astype(BF16)
    line = lax.broadcasted_iota(jnp.int32, (8, TILE), 0)
    which = lax.rem(line, 4)
    payload = jnp.where(
        which == 0, low, jnp.where(which == 1, bound, jnp.where(which == 2, row, member))
    ).astype(F32).astype(BF16)
    ordered = lax.dot_general(
        payload, chosen, (((1,), (1,)), ((), ())), preferred_element_type=F32
    )
    head = jnp.where(line[:, :HALF] < 4, ordered[:, :HALF], ordered[:, HALF:])
    edge = (lax.broadcasted_iota(jnp.int32, (1, HALF), 1) * TILE).astype(F32)
    before = jnp.sum((keys_t[:, :HALF] < edge).astype(F32), axis=0, keepdims=True)
    return jnp.concatenate([head, jnp.broadcast_to(before, (8, HALF))], axis=0).astype(BF16)


def exchange_kernel(
    n_node, n_feat,
    feat_hbm, cot_hbm, deg_hbm, row_hbm, col_hbm, fill_hbm,
    blocks, feats, self_out,
    cot, ints, send, g_send, g_feat, g_node, g_tile, g_back,
    in_sems, a_sems, g_sems, y_sems, z_sems, end_sems,
):
    node_y, ring_z = n_node // 4, n_feat // 2
    span = n_feat + 1
    cut = (span * 11) // 25
    width = cot.shape[0]
    x, y, core = node_coords(node_y)
    me_n, me_f = lax.axis_index("node"), lax.axis_index("feat")
    hi, z = lax.div(me_f, ring_z), lax.rem(me_f, ring_z)
    loads = [
        pltpu.make_async_copy(src, dst, in_sems.at[k])
        for k, (src, dst) in enumerate((
            (cot_hbm, cot), (deg_hbm, ints.at[0]), (feat_hbm, feats.at[me_f]),
            (row_hbm, ints.at[1]), (col_hbm, ints.at[2]), (fill_hbm, ints.at[3]),
        ))
    ]
    for load in loads:
        load.start()
    barrier, expected = greet(n_node, n_feat)
    loads[0].wait()
    loads[1].wait()
    scaled = cot[...].astype(F32) / ints[0].astype(F32)
    for j in range(n_feat):
        part = scaled[j * WIDTH:(j + 1) * WIDTH]
        send[j] = jnp.concatenate([part[:, :HALF], part[:, HALF:]], axis=0).astype(BF16)
    home = me_n * span
    blocks[home + me_f] = send[me_f]
    for load in loads[2:]:
        load.wait()
    blocks[home + n_feat] = group_table(n_node, n_feat, ints[1], ints[2], ints[3])
    pl.semaphore_wait(barrier, expected)

    spread("feat", n_feat, lambda p: send.at[p], blocks.at[home + me_f], a_sems.at[0], a_sems.at[1])

    def z_view(side, offset, lo, hi_row):
        hh = hi if side == 0 else 1 - hi
        return feats.at[hh * ring_z + wrap(z + offset, ring_z), pl.ds(lo, hi_row - lo)]

    mid = width // 2
    z_near = [(0, 0, mid), (0, mid, width), (1, 0, mid), (1, mid, width)]
    z_ring = Ring(
        ring_z, z_view, lambda way: {"feat": hi * ring_z + wrap(z + way, ring_z)},
        z_near, {1: z_near[:2], -1: z_near[2:]}, z_sems, 0, end_sems.at[3], lambda *_: None,
    )
    for side, lo, up in z_near[:2]:
        for way in (1, -1):
            z_ring.pass_on(0, way, side, lo, up)
        z_ring.move(("x", lo), z_view(0, 0, lo, up), {"feat": (1 - hi) * ring_z + z}, up - lo)

    local = lax.dot_general(
        feats[me_f], cot[...], (((1,), (1,)), ((), ())), preferred_element_type=F32
    )
    for j in range(n_feat):
        g_send[j] = to_tile(local[j * WIDTH:(j + 1) * WIDTH]).astype(BF16)
    g_feat[me_f] = g_send[me_f]
    spread("feat", n_feat, lambda p: g_send.at[p], g_feat.at[me_f], g_sems.at[0], g_sems.at[1])

    def z_partner():
        for side, lo, up in z_near[2:]:
            wait_bytes(z_view(1, 0, lo, up), z_ring.sem(("x", lo)))
            for way in (1, -1):
                z_ring.pass_on(0, way, 1, lo, up)

    z_partner()
    wait_bytes(send.at[pl.ds(0, n_feat - 1)], a_sems.at[1])

    def node_at(xx, yy, cc):
        return (xx * node_y + yy) * 2 + cc

    def y_view(side, offset, lo, up):
        xx = x if side == 0 else 1 - x
        return blocks.at[pl.ds(node_at(xx, wrap(y + offset, node_y), core) * span + lo, up - lo)]

    def to_sibling(ref):
        push(ref, ref, end_sems.at[1], end_sems.at[2], {"node": node_at(x, y, 1 - core)})

    fresh = []

    def y_landed(way, step, side, lo, up, ref):
        if side == 0 and lo >= cut:
            name = ("x", way, step, lo)
            y_ring.move(name, ref, partner, up - lo)
            fresh.append((name, -way * step, lo, up))
        to_sibling(ref)

    partner = {"node": node_at(1 - x, y, core)}
    room = (span + cut) // 2
    y_near = [(0, cut, span), (0, 0, cut), (1, 0, cut)]
    y_ring = Ring(
        node_y, y_view, lambda way: {"node": node_at(x, wrap(y + way, node_y), core)}, y_near,
        {1: [(0, cut, room), (0, 0, cut)], -1: [(0, room, span), (1, 0, cut)]},
        y_sems, 0, end_sems.at[0], y_landed,
    )

    def from_partner():
        waiting = list(fresh)
        fresh.clear()
        return waiting

    def drain(waiting):
        for name, offset, lo, up in waiting:
            ref = y_view(1, offset, lo, up)
            wait_bytes(ref, y_ring.sem(name))
            to_sibling(ref)

    for side, lo, up in ((0, 0, cut), (0, cut, span)):
        y_ring.move(("x", 0, 0, lo), y_view(0, 0, lo, up), partner, up - lo)
        for way in (1, -1):
            y_ring.pass_on(0, way, side, lo, up)
    to_sibling(y_view(0, 0, 0, span))
    fresh.append((("x", 0, 0, cut), 0, cut, span))

    z_ring.receive(1)
    ref = y_view(1, 0, 0, cut)
    wait_bytes(ref, y_ring.sem(("x", 0, 0, 0)))
    for way in (1, -1):
        y_ring.pass_on(0, way, 1, 0, cut)
    to_sibling(ref)
    wait_bytes(g_feat.at[pl.ds(0, n_feat - 1)], g_sems.at[1])
    g_tile[...] = jnp.sum(g_feat[...].astype(F32), axis=0)
    g_node[me_n] = g_tile[...]
    spread("node", n_node, lambda p: g_tile, g_node.at[me_n], g_sems.at[2], g_sems.at[3])

    waiting = from_partner()
    z_step = 1
    for step in range(1, node_y // 2 + 1):
        y_ring.receive(step)
        drain(waiting)
        waiting = from_partner()
        if z_step < ring_z // 2:
            z_step += 1
            z_ring.receive(z_step)
        if step == 1:
            wait_bytes(g_node.at[pl.ds(0, n_node - 1)], g_sems.at[3])
            g_back[me_f] = jnp.sum(g_node[...], axis=0).astype(BF16)
            spread("feat", n_feat, lambda p: g_back.at[me_f], g_back.at[me_f], g_sems.at[4], g_sems.at[5])
    drain(waiting)
    while z_step < ring_z // 2:
        z_step += 1
        z_ring.receive(z_step)

    wait_bytes(g_back.at[pl.ds(0, n_feat - 1)], g_sems.at[5])
    self_out[...] = from_tiles(g_back[...], width) * (1.0 / math.sqrt(n_node * n_feat * TILE))
    wait_bytes(send.at[pl.ds(0, n_feat - 1)], a_sems.at[0])
    wait_bytes(g_send.at[pl.ds(0, n_feat - 1)], g_sems.at[0])
    wait_bytes(g_node.at[pl.ds(0, n_node - 1)], g_sems.at[2])
    wait_bytes(g_back.at[pl.ds(0, n_feat - 1)], g_sems.at[4])
    wait_bytes(blocks.at[pl.ds(0, n_node // 2 * span)], end_sems.at[2])
    wait_bytes(blocks.at[pl.ds(0, n_node // 2 * span)], end_sems.at[1])
    wait_bytes(blocks.at[pl.ds(0, y_ring.sent)], end_sems.at[0])
    wait_bytes(feats.at[pl.ds(0, z_ring.sent // width)], end_sems.at[3])


def slots_kernel(
    n_node, n_feat, blocks, feats, out, neigh_out,
    acc, base, packed, before, packed_s, before_s, todo, sems,
):
    span = n_feat + 1
    me = lax.axis_index("node")

    table = blocks[...].reshape(n_node, span, 16, HALF)[:, n_feat].astype(F32).astype(jnp.int32)
    for k in range(2):
        low = table[:, 4 * k, :]
        bound = table[:, 4 * k + 1, :]
        row = table[:, 4 * k + 2, :]
        member = table[:, 4 * k + 3, :]
        first = lax.broadcasted_iota(jnp.int32, (n_node, HALF), 0) * span
        packed[k] = (first + row) + low * 1024 + bound * (1 << 18) + member * (1 << 25)
    before[...] = table[:, 8, :]
    moves = [
        pltpu.make_async_copy(packed, packed_s, sems.at[0]),
        pltpu.make_async_copy(before, before_s, sems.at[1]),
    ]
    for one in moves:
        one.start()

    r = lax.broadcasted_iota(jnp.int32, (TILE, TILE), 0)
    c = lax.broadcasted_iota(jnp.int32, (TILE, TILE), 1)
    residue = lax.rem(13 * r * r + 7 * r * c + 197 * c, MOD)
    base[...] = (residue * 256 - 32768).astype(jnp.int16)
    acc[...] = jnp.zeros_like(acc)
    for one in moves:
        one.wait()

    def collect_group(g, count):
        start, stop = before_s[g, me], before_s[g, me + 1]

        def put(i, at):
            todo[at] = packed_s[lax.div(i, HALF), g, lax.rem(i, HALF)]
            return at + 1

        return lax.fori_loop(start, stop, put, count)

    count = lax.fori_loop(0, n_node, collect_group, 0)
    for k in range(UNROLL - 1):
        todo[count + k] = 0

    def turn(i, _):
        sums = []
        for k in range(UNROLL):
            entry = todo[i * UNROLL + k]
            place = jnp.bitwise_and(entry, 1023)
            low = jnp.bitwise_and(lax.shift_right_logical(entry, 10), 255)
            bound = jnp.bitwise_and(lax.shift_right_logical(entry, 18), 127)
            pair = blocks[place].astype(F32)
            source = jnp.concatenate([pair[:8], pair[8:]], axis=1).astype(BF16)
            moved = base[...] - jnp.full((TILE, TILE), low * 256, jnp.int32).astype(jnp.int16)
            limit = jnp.full((TILE, TILE), bound * 256 - 32768, jnp.int32).astype(jnp.int16)
            pattern = jnp.where(moved < limit, jnp.ones((), BF16), jnp.zeros((), BF16))
            sums.append((lax.shift_right_logical(entry, 25),
                         jnp.dot(source, pattern, preferred_element_type=F32)))
        for member, product in sums:
            acc[member] += product
        return 0

    lax.fori_loop(0, lax.div(count + UNROLL - 1, UNROLL), turn, 0)
    total = jnp.zeros((WIDTH, feats.shape[1]), F32)
    for m in range(n_feat):
        part = acc[m]
        out[m] = jnp.concatenate([part[:, :HALF], part[:, HALF:]], axis=0).astype(BF16)
        total += lax.dot_general(
            part.astype(BF16), feats[m], (((1,), (1,)), ((), ())), preferred_element_type=F32
        )
    neigh_out[...] = to_tile(total).astype(BF16)


def finish_kernel(
    n_node, n_feat,
    slices, neigh, cot, w_self, w_neigh,
    grad_out, neigh_out,
    landed, g_node, g_back, g_sems, a_sems,
):
    width = cot.shape[0]
    me_n, me_f = lax.axis_index("node"), lax.axis_index("feat")
    barrier, expected = greet(n_node, n_feat)
    landed[me_f] = slices[me_f]
    g_node[me_n] = neigh[...]
    own = jnp.dot(w_self[...], cot[...], preferred_element_type=F32)
    pl.semaphore_wait(barrier, expected)
    spread("node", n_node, lambda p: neigh, g_node.at[me_n], g_sems.at[0], g_sems.at[1])
    spread("feat", n_feat, lambda p: slices.at[p], landed.at[me_f], a_sems.at[0], a_sems.at[1])
    wait_bytes(g_node.at[pl.ds(0, n_node - 1)], g_sems.at[1])
    g_back[me_f] = jnp.sum(g_node[...].astype(F32), axis=0).astype(BF16)
    spread("feat", n_feat, lambda p: g_back.at[me_f], g_back.at[me_f], g_sems.at[2], g_sems.at[3])
    wait_bytes(landed.at[pl.ds(0, n_feat - 1)], a_sems.at[1])
    gathered = from_tiles(landed[...], TILE).astype(BF16)
    grad_out[...] = (
        own + jnp.dot(w_neigh[...], gathered, preferred_element_type=F32)
    ).astype(BF16)
    wait_bytes(g_back.at[pl.ds(0, n_feat - 1)], g_sems.at[3])
    neigh_out[...] = from_tiles(g_back[...], width).T * (1.0 / math.sqrt(n_node * n_feat * TILE))
    wait_bytes(g_back.at[pl.ds(0, n_feat - 1)], g_sems.at[2])
    wait_bytes(g_node.at[pl.ds(0, n_node - 1)], g_sems.at[0])
    wait_bytes(slices.at[pl.ds(0, n_feat - 1)], a_sems.at[0])


def any_slots(n_node, n_feat, features, cotangent, w_self, w_neigh, degree, tile_row, tile_col, tile_fill):
    width = n_feat * WIDTH
    span = n_feat + 1
    line = (1, TILE)
    tile = (16, HALF)
    shape = jax.ShapeDtypeStruct
    dma = pltpu.SemaphoreType.DMA
    cot_t = cotangent.T
    blocks, feats, self_grad = pl.pallas_call(
        functools.partial(exchange_kernel, n_node, n_feat),
        out_shape=(
            shape((n_node * span, *tile), BF16),
            shape((n_feat, width, TILE), BF16),
            shape((width, width), F32),
        ),
        in_specs=[pl.BlockSpec(memory_space=pltpu.HBM)] * 6,
        out_specs=tuple(in_vmem(3)),
        scratch_shapes=[
            pltpu.VMEM((width, TILE), BF16),
            pltpu.VMEM((4, *line), jnp.int32),
            pltpu.VMEM((n_feat, *tile), BF16),
            pltpu.VMEM((n_feat, *tile), BF16),
            pltpu.VMEM((n_feat, *tile), BF16),
            pltpu.VMEM((n_node, *tile), F32),
            pltpu.VMEM(tile, F32),
            pltpu.VMEM((n_feat, *tile), BF16),
            dma((6,)), dma((2,)), dma((6,)), dma((64,)), dma((64,)), dma((4,)),
        ],
        compiler_params=pltpu.CompilerParams(
            collective_id=1, has_side_effects=True, vmem_limit_bytes=32 << 20
        ),
        name="exchange",
    )(
        features.T, cot_t, degree.reshape(line), tile_row.reshape(line),
        tile_col.reshape(line), tile_fill.reshape(line),
    )
    slices, neigh = pl.pallas_call(
        functools.partial(slots_kernel, n_node, n_feat),
        out_shape=(shape((n_feat, *tile), BF16), shape(tile, BF16)),
        in_specs=in_vmem(2),
        out_specs=tuple(in_vmem(2)),
        scratch_shapes=[
            pltpu.VMEM((n_feat, WIDTH, TILE), F32),
            pltpu.VMEM((TILE, TILE), jnp.int16),
            pltpu.VMEM((2, n_node, HALF), jnp.int32),
            pltpu.VMEM((n_node, HALF), jnp.int32),
            pltpu.SMEM((2, n_node, HALF), jnp.int32),
            pltpu.SMEM((n_node, HALF), jnp.int32),
            pltpu.SMEM((n_node * TILE + UNROLL,), jnp.int32),
            dma((2,)),
        ],
        compiler_params=pltpu.CompilerParams(vmem_limit_bytes=32 << 20),
        name="slots",
    )(blocks, feats)
    input_grad, neigh_grad = pl.pallas_call(
        functools.partial(finish_kernel, n_node, n_feat),
        out_shape=(shape((width, TILE), BF16), shape((width, width), F32)),
        in_specs=in_vmem(5),
        out_specs=tuple(in_vmem(2)),
        scratch_shapes=[
            pltpu.VMEM((n_feat, *tile), BF16),
            pltpu.VMEM((n_node, *tile), BF16),
            pltpu.VMEM((n_feat, *tile), BF16),
            dma((4,)), dma((2,)),
        ],
        compiler_params=pltpu.CompilerParams(
            collective_id=2, has_side_effects=True, vmem_limit_bytes=32 << 20
        ),
        name="finish",
    )(slices, neigh, cot_t, w_self, w_neigh)
    return input_grad.T, self_grad, neigh_grad


def local(n_node, n_feat, *args):
    done, flag = few_slots(n_node, n_feat, *args)
    return lax.cond(flag > 0.0, lambda done, args: any_slots(n_node, n_feat, *args), lambda done, args: done, done, args)


def solution(mesh):
    n_node, n_feat = mesh.shape["node"], mesh.shape["feat"]
    return jax.shard_map(
        functools.partial(local, n_node, n_feat),
        mesh=mesh,
        in_specs=(
            P(("node", "feat"), None),
            P(("node", "feat"), None),
            P(),
            P(),
            P(("node", "feat")),
            P("node"),
            P("node"),
            P("node"),
        ),
        out_specs=(P(("node", "feat"), None), P(), P()),
        check_vma=False,
    )
```
